256 devices in a mesh: dp: 32 (over y, z), head: 8 (over x, core).
Axes of the slice: x: 4, y: 4, z: 8, core: 2. Of those that a mesh axis runs over, the one named last changes fastest.
Arguments:
- queries: bfloat16 [32768, 8192], P('dp', 'head'), parts along dimension 1
- key_rows: bfloat16 [32768, 1024], P('dp', 'head'), parts along dimension 1, as said below
- value_rows: bfloat16 [32768, 1024], P('dp', 'head'), parts along dimension 1, may hold values from -6 to 6
- out_grads: bfloat16 [32768, 8192], P('dp', 'head'), parts along dimension 1, may hold values from -6 to 6
- block_docs: int32 [32, 8], replicated, may hold values from 0 to 7, as said below
- moved_blocks: int32 [32], replicated, may hold values from 1 to 7, as said below
Outputs:
- attended: bfloat16 [32768, 8192], P('dp', 'head'), parts along dimension 1
- query_grad: bfloat16 [32768, 8192], P('dp', 'head'), parts along dimension 1
- key_grad: bfloat16 [32768, 1024], P('dp', 'head'), parts along dimension 1
- value_grad: bfloat16 [32768, 1024], P('dp', 'head'), parts along dimension 1
The draws below stay inside these ranges and needn't reach their ends.
There are 8 independent parts, one for each index of `head`. The reference program is written for one: setup_inputs(seed, part) draws one part's arguments, and reference() takes and returns one part's arrays. A program takes and returns all parts, laid end to end along the dimension named above; an argument that names none is the same for every part. Nothing has to cross between parts.
Inputs may be any that keep to these rules, and one draw needn't show every extreme that they name: `key_rows`: custom draw of keys. `block_docs`: each row starts at 0 and rises by 0 or 1 from block to block; in row r a new document begins at block moved_blocks[r]. moved_blocks[r] equals moved_blocks[(r + 16) % 32].
All inputs are finite; a program needn't handle non-finite values.
Results may differ from the reference program's by a relative error of at most 0.005.
Values may be sent and summed in bfloat16 or wider, within the bound.
No kernel may reach another device: no remote copies, remote signals or barrier semaphores. Data moves between devices by JAX's collectives and lax.ppermute only.
A program may use at most 128 MiB of HBM per device.

```python
import math
import jax
import jax.numpy as jnp
from jax import lax

HQ = 8
HD = 128
NB = 8
BLK = 128
TOKENS = 32768
N_DP = 32


def drawn_pair(key):
    base_q = jnp.clip(jax.random.normal(jax.random.fold_in(key, 11), (TOKENS, HQ * HD), jnp.float32), -6.0, 6.0)
    base_k = jnp.clip(jax.random.normal(jax.random.fold_in(key, 12), (TOKENS, HD), jnp.float32), -4.5, 4.5)
    return (base_q, base_k)


def draw_queries(key, part):
    base_q, base_k = drawn_pair(key)
    return base_q.astype(jnp.bfloat16)


def draw_key_rows(key, part):
    base_q, base_k = drawn_pair(key)
    return base_k.astype(jnp.bfloat16)


def document_plan(key):
    pairs = N_DP // 2
    counts = jax.random.randint(jax.random.fold_in(key, 21), (pairs,), 1, NB)
    counts = counts.at[0].set(NB - 1).at[1].set(1)
    replica = lax.iota(jnp.int32, N_DP)
    moved = counts[replica % pairs]
    starts = jax.random.randint(jax.random.fold_in(key, 22), (N_DP, NB), 0, 2)
    column = lax.iota(jnp.int32, NB)[None, :]
    starts = jnp.where((column == 0) | (column == moved[:, None]) | (replica[:, None] == 0), 1, starts)
    documents = jnp.cumsum(starts, axis=1) - 1
    return (documents.astype(jnp.int32), moved.astype(jnp.int32))


def draw_block_docs(key, part):
    return document_plan(key)[0]


def draw_moved_blocks(key, part):
    return document_plan(key)[1]


def steps_of(rng, shape, cuts, least, high):
    level = 1.0
    for axis_at, blocks in cuts:
        heights = jax.random.uniform(jax.random.fold_in(jax.random.fold_in(rng, 6), axis_at), (blocks,), jnp.float32, least / len(cuts), high / len(cuts))
        level = level * jnp.repeat(jnp.exp(heights), shape[axis_at] // blocks).reshape((-1,) + (1,) * (len(shape) - 1 - axis_at))
    return level


def scatter_about(rng, dims, scale, reach, pieces=(), dtype=jnp.bfloat16):
    factor_of = steps_of(rng, dims, pieces, -0.22, 0.18) if pieces else 1.0
    values = jax.random.normal(rng, dims, jnp.float32) * scale * factor_of
    return jnp.minimum(jnp.maximum(values, -reach), reach).astype(dtype)


def setup_inputs(seed: int = 0, part: int = 0) -> dict:
    key_list = jax.random.split(jax.random.key(seed), 7)
    part_splits = jax.random.split(jax.random.fold_in(key_list[6], part), 7)
    return {
        "queries": draw_queries(jax.random.fold_in(jax.random.fold_in(key_list[6], part), 71), part),
        "key_rows": draw_key_rows(jax.random.fold_in(jax.random.fold_in(key_list[6], part), 71), part),
        "value_rows": scatter_about(part_splits[2], (TOKENS, HD), 1.0, 6.0, ((0, 32),)),
        "out_grads": scatter_about(part_splits[3], (TOKENS, HQ * HD), 1.0, 6.0, ((0, 32),)),
        "block_docs": draw_block_docs(jax.random.fold_in(key_list[6], 71), part),
        "moved_blocks": draw_moved_blocks(jax.random.fold_in(key_list[6], 71), part),
    }


def head_pass(query_head, grad_head, key_rows, value_rows, allowed):
    factor = 1.0 / math.sqrt(key_rows.shape[1])
    scores = jnp.dot(query_head, key_rows.T, preferred_element_type=jnp.float32) * factor
    scores = jnp.where(allowed, scores, -jnp.inf)
    highest = lax.optimization_barrier(jnp.max(scores, axis=1, keepdims=True))
    weights = jnp.exp(scores - highest)
    attention = weights / lax.optimization_barrier(jnp.sum(weights, axis=1, keepdims=True))
    attention_low = attention.astype(jnp.bfloat16)
    attended = jnp.dot(attention_low, value_rows, preferred_element_type=jnp.float32)
    dprobs = jnp.dot(grad_head, value_rows.T, preferred_element_type=jnp.float32)
    centre = lax.optimization_barrier(jnp.sum(attention * dprobs, axis=1, keepdims=True))
    dscores = (attention * (dprobs - centre)).astype(jnp.bfloat16)
    query_grad = jnp.dot(dscores, key_rows, preferred_element_type=jnp.float32) * factor
    key_grad = jnp.dot(dscores.T, query_head, preferred_element_type=jnp.float32) * factor
    value_grad = jnp.dot(attention_low.T, grad_head, preferred_element_type=jnp.float32)
    return (attended.astype(jnp.bfloat16), query_grad.astype(jnp.bfloat16), key_grad, value_grad)

def attend(queries, key_rows, value_rows, out_grads, documents):
    count = key_rows.shape[0]
    width = key_rows.shape[1]
    heads = queries.shape[1] // width
    places = lax.iota(jnp.int32, count)
    allowed = (documents[:, None] == documents[None, :]) & (places[None, :] <= places[:, None])
    split_query = jnp.transpose(queries.reshape(count, heads, width), (1, 0, 2))
    split_grad = jnp.transpose(out_grads.reshape(count, heads, width), (1, 0, 2))

    def one_head(items):
        return head_pass(items[0], items[1], key_rows, value_rows, allowed)
    attended, query_grad, key_grad, value_grad = lax.map(one_head, (split_query, split_grad))

    def merged(array):
        return jnp.transpose(array, (1, 0, 2)).reshape(count, heads * width)
    return (merged(attended), merged(query_grad), lax.optimization_barrier(jnp.sum(key_grad, axis=0)).astype(jnp.bfloat16), lax.optimization_barrier(jnp.sum(value_grad, axis=0)).astype(jnp.bfloat16))

def rehome(own, other, offset):
    count = own.shape[0]
    places = lax.iota(jnp.int32, count).reshape((count,) + (1,) * (own.ndim - 1))
    front = jnp.roll(own, -offset, axis=0)
    back = jnp.roll(other, count - offset, axis=0)
    return jnp.where(places < count - offset, front, back)

def reference(queries, key_rows, value_rows, out_grads, block_docs, moved_blocks):
    count = NB * BLK

    def split(array):
        return array.reshape(N_DP, count, array.shape[1])
    documents = jnp.repeat(block_docs, BLK, axis=1)

    def replica_pass(items):
        return attend(items[0], items[1], items[2], items[3], items[4])
    results = lax.map(replica_pass, (split(queries), split(key_rows), split(value_rows), split(out_grads), documents))
    offsets = moved_blocks * BLK

    def placed(array):
        return jax.vmap(rehome)(array, jnp.roll(array, N_DP // 2, axis=0), offsets).reshape(N_DP * count, array.shape[2])
    return (placed(results[0]), placed(results[1]), placed(results[2]), placed(results[3]))
```

```python
import functools
import math

import jax
import jax.numpy as jnp
from jax import lax
from jax.experimental import pallas as pl
from jax.experimental.pallas import tpu as pltpu
from jax.sharding import PartitionSpec as P

NB = 8
BLK = 128
HQ = 8
HD = 128
WIDE = HQ * HD
ROWS = NB * BLK
GROUPS = {1: 4, 2: 4, 3: 2, 4: 2, 5: 2, 6: 2, 7: 2}
FACTOR = 1.0 / math.sqrt(HD)
LOG_FACTOR = FACTOR * math.log2(math.e)
VMEM_BYTES = 63 * 1024 * 1024


def dot(a, b, contract):
    return lax.dot_general(a, b, ((contract[:1], contract[1:]), ((), ())), preferred_element_type=jnp.float32)


def block_range(position, block, docs_ref):
    document = docs_ref[block, position]
    same = jnp.int32(0)
    for other in range(NB):
        hit = (docs_ref[other, position] == document) & (other <= block)
        same = same + jnp.where(hit, 1, 0)
    return same


def stacked(ref, head, group):
    columns = [pl.ds(pl.multiple_of((head + g) * HD, HD), HD) for g in range(group)]
    return jnp.concatenate([ref[:, at] for at in columns], axis=0)


def attend_block(blocks, begin, refs, write):
    q_ref, g_ref, k_ref, v_ref, kt_ref, vt_ref, dk_ref, dv_ref = refs
    width = blocks * BLK
    group = GROUPS[blocks]
    columns = group * BLK
    span = pl.ds(begin, width)

    def heads(turn, _):
        head = turn * group
        query = stacked(q_ref, head, group)
        grad = stacked(g_ref, head, group)
        key_place = lax.broadcasted_iota(jnp.int32, (BLK, columns), 0)
        query_place = lax.rem(lax.broadcasted_iota(jnp.int32, (BLK, columns), 1), BLK)
        scores = dot(k_ref[span, :], query, (1, 1))
        last = jnp.where(key_place <= query_place, scores[width - BLK :], -jnp.inf)
        scores = last if blocks == 1 else jnp.concatenate([scores[: width - BLK], last], axis=0)
        highest = jnp.max(scores, axis=0, keepdims=True)
        weights = jnp.exp2((scores - highest) * LOG_FACTOR)
        probs = weights * (1.0 / jnp.sum(weights, axis=0, keepdims=True))
        probs_low = probs.astype(jnp.bfloat16)
        dprobs = dot(v_ref[span, :], grad, (1, 1))
        centre = jnp.sum(probs * dprobs, axis=0, keepdims=True)
        dscores = (probs * (dprobs - centre)).astype(jnp.bfloat16)
        attended = dot(vt_ref[:, span], probs_low, (1, 0)).T.astype(jnp.bfloat16)
        query_grad = (dot(kt_ref[:, span], dscores, (1, 0)) * FACTOR).T.astype(jnp.bfloat16)
        for g in range(group):
            write(head + g, attended[g * BLK : (g + 1) * BLK], query_grad[g * BLK : (g + 1) * BLK])
        dk_ref[span, :] += dot(dscores, query, (1, 0))
        dv_ref[span, :] += dot(probs_low, grad, (1, 0))
        return 0

    lax.fori_loop(0, HQ // group, heads, 0)


def dispatch(block, most, same, refs, write):
    for blocks in range(1, most + 1):

        @pl.when(same == blocks)
        def _(blocks=blocks):
            begin = pl.multiple_of((block + 1 - blocks) * BLK, BLK)
            attend_block(blocks, begin, refs, write)


EARLY = 2
FULL = 5
EXTRA = tuple(range(FULL, NB - 1))


def first_kernel(pos_ref, docs_ref, q_ref, g_ref, k_ref, v_ref, send_ref, dk_out, dv_out, kt, vt):
    block = pl.program_id(0)

    @pl.when(block == 0)
    def _():
        kt[...] = k_ref[...].T
        vt[...] = v_ref[...].T
        dk_out[...] = jnp.zeros_like(dk_out)
        dv_out[...] = jnp.zeros_like(dv_out)

    def write(head, attended, query_grad):
        send_ref[:, pl.ds(pl.multiple_of(head * HD, HD), HD)] = attended
        send_ref[:, pl.ds(pl.multiple_of(WIDE + head * HD, HD), HD)] = query_grad

    same = block_range(pos_ref[0], block, docs_ref)
    dispatch(block, EARLY, same, (q_ref, g_ref, k_ref, v_ref, kt, vt, dk_out, dv_out), write)


def first_blocks(position, docs, q, k, v, g):
    whole = lambda rows, columns: pl.BlockSpec((rows, columns), lambda i, *_: (0, 0))
    row = lambda columns: pl.BlockSpec((BLK, columns), lambda i, *_: (i, 0))
    rows = EARLY * BLK
    return pl.pallas_call(
        first_kernel,
        grid_spec=pltpu.PrefetchScalarGridSpec(
            num_scalar_prefetch=2,
            grid=(EARLY,),
            in_specs=[row(WIDE), row(WIDE), whole(rows, HD), whole(rows, HD)],
            out_specs=[row(2 * WIDE), whole(rows, HD), whole(rows, HD)],
            scratch_shapes=[pltpu.VMEM((HD, rows), jnp.bfloat16)] * 2,
        ),
        out_shape=[
            jax.ShapeDtypeStruct((rows, 2 * WIDE), jnp.bfloat16),
            jax.ShapeDtypeStruct((rows, HD), jnp.float32),
            jax.ShapeDtypeStruct((rows, HD), jnp.float32),
        ],
        compiler_params=pltpu.CompilerParams(vmem_limit_bytes=VMEM_BYTES),
        cost_estimate=pl.CostEstimate(flops=2 * 18 * HQ * BLK * BLK * HD, bytes_accessed=8 * BLK * WIDE * 2, transcendentals=0),
        name="first_blocks",
    )(position, docs, q, g, k, v)


def rest_kernel(pos_ref, docs_ref, moved_ref, q_ref, g_ref, k_ref, v_ref, early_ref, dk0_ref, dv0_ref, *rest):
    main_ref, small_ref, *extras = rest[: 2 + len(EXTRA)]
    att_ref, dq_ref, dk_fin, dv_fin, kt, vt, dk_ref, dv_ref = rest[2 + len(EXTRA) :]
    step = pl.program_id(0)
    block = step + 1
    position = pos_ref[0]
    moved = moved_ref[position]

    @pl.when(step == 0)
    def _():
        kt[...] = k_ref[...].T
        vt[...] = v_ref[...].T
        dk_ref[...] = jnp.zeros_like(dk_ref)
        dv_ref[...] = jnp.zeros_like(dv_ref)
        dk_ref[: EARLY * BLK] = dk0_ref[...]
        dv_ref[: EARLY * BLK] = dv0_ref[...]
        att_ref[...] = early_ref[:, :WIDE]
        dq_ref[...] = early_ref[:, WIDE:]

    def write(head, attended, query_grad):
        here = pl.ds(pl.multiple_of(head * HD, HD), HD)
        att_ref[:, here] = attended
        dq_ref[:, here] = query_grad

    @pl.when(step > 0)
    def _():
        same = block_range(position, block, docs_ref)
        dispatch(block, NB - 1, same, (q_ref, g_ref, k_ref, v_ref, kt, vt, dk_ref, dv_ref), write)

    for at in range(EARLY, NB - 1):

        @pl.when((block == at) & (at < moved))
        def _(at=at):
            if at < FULL:
                ref, rows = main_ref, slice((at - EARLY) * BLK, (at - EARLY + 1) * BLK)
            else:
                ref, rows = extras[at - FULL], slice(0, BLK)
            ref[rows, :WIDE] = att_ref[...]
            ref[rows, WIDE : 2 * WIDE] = dq_ref[...]

    @pl.when(step == NB - 2)
    def _():
        for at in range(NB):
            rows = slice(at * BLK, (at + 1) * BLK)
            dk = (dk_ref[rows] * FACTOR).astype(jnp.bfloat16)
            dv = dv_ref[rows].astype(jnp.bfloat16)
            if at < NB - 1:
                if at < EARLY:
                    ref, to, column = small_ref, rows, 0
                elif at < FULL:
                    ref, to, column = main_ref, slice((at - EARLY) * BLK, (at - EARLY + 1) * BLK), 2 * WIDE
                else:
                    ref, to, column = extras[at - FULL], slice(0, BLK), 2 * WIDE
                ref[to, column : column + HD] = dk
                ref[to, column + HD : column + 2 * HD] = dv
            if at > 0:

                @pl.when(at >= moved)
                def _():
                    to = pl.ds(pl.multiple_of((at - moved) * BLK, BLK), BLK)
                    dk_fin[to, :] = dk
                    dv_fin[to, :] = dv


PARCELS = [
    jax.ShapeDtypeStruct(((FULL - EARLY) * BLK, 2 * WIDE + 2 * HD), jnp.bfloat16),
    jax.ShapeDtypeStruct((EARLY * BLK, 2 * HD), jnp.bfloat16),
] + [jax.ShapeDtypeStruct((BLK, 2 * WIDE + 2 * HD), jnp.bfloat16)] * len(EXTRA)
RESULTS = [jax.ShapeDtypeStruct((ROWS, columns), jnp.bfloat16) for columns in (WIDE, WIDE, HD, HD)]


def rest_blocks(position, docs, moved, q, k, v, g, early, dk0, dv0):
    def stay(i, pos, docs, moved):
        return (jnp.maximum(i + 1 - moved[pos[0]], 0), 0)

    whole = lambda rows, columns: pl.BlockSpec((rows, columns), lambda i, *_: (0, 0))
    row = pl.BlockSpec((BLK, WIDE), lambda i, *_: (jnp.maximum(i + 1, EARLY), 0))
    early_row = pl.BlockSpec((BLK, 2 * WIDE), lambda i, *_: (1, 0))
    return pl.pallas_call(
        rest_kernel,
        grid_spec=pltpu.PrefetchScalarGridSpec(
            num_scalar_prefetch=3,
            grid=(NB - 1,),
            in_specs=[row, row, whole(ROWS, HD), whole(ROWS, HD), early_row, whole(EARLY * BLK, HD), whole(EARLY * BLK, HD)],
            out_specs=[whole(*parcel.shape) for parcel in PARCELS]
            + [
                pl.BlockSpec((BLK, WIDE), stay),
                pl.BlockSpec((BLK, WIDE), stay),
                whole(ROWS, HD),
                whole(ROWS, HD),
            ],
            scratch_shapes=[pltpu.VMEM((HD, ROWS), jnp.bfloat16)] * 2 + [pltpu.VMEM((ROWS, HD), jnp.float32)] * 2,
        ),
        out_shape=[pltpu.HBM(parcel.shape, parcel.dtype) for parcel in PARCELS] + RESULTS,
        compiler_params=pltpu.CompilerParams(vmem_limit_bytes=VMEM_BYTES),
        cost_estimate=pl.CostEstimate(flops=2 * 6 * HQ * BLK * BLK * HD * 20, bytes_accessed=8 * ROWS * WIDE, transcendentals=0),
        name="rest_blocks",
    )(position, docs, moved, q, g, k, v, early, dk0, dv0)


LANES = 8


def route_of(position, moved_ref):
    lane = lax.rem(position, LANES)
    base = lax.rem(position, 2 * LANES) - lane
    load = [moved_ref[base + z] for z in range(LANES)]
    ranks = []
    for z in range(LANES):
        rank = jnp.int32(0)
        for other in range(LANES):
            if other != z:
                ahead = load[other] >= load[z] if other < z else load[other] > load[z]
                rank = rank + jnp.where(ahead, 1, 0)
        ranks.append(rank)
    mine = jnp.int32(0)
    for z in range(LANES):
        mine = mine + jnp.where(lane == z, ranks[z], 0)
    top = jnp.minimum(mine, LANES - 1 - mine)
    heavy = light = most = least = jnp.int32(0)
    for z in range(LANES):
        heavy = heavy + jnp.where(ranks[z] == top, z, 0)
        light = light + jnp.where(ranks[z] == LANES - 1 - top, z, 0)
        most = most + jnp.where(ranks[z] == top, load[z], 0)
        least = least + jnp.where(ranks[z] == LANES - 1 - top, load[z], 0)
    step = heavy ^ light
    bit = jnp.where(step >= 4, 4, jnp.where(step >= 2, 2, 1))
    side = jnp.where((heavy & bit) != 0, 1, 0)
    relayed = (most == NB - 1) & (least <= FULL)
    return jnp.where(relayed, 3 + (step - 1) * 2 + side, jnp.maximum(most, FULL) - FULL)


def place_kernel(pos_ref, moved_ref, early_ref, main_ref, small_ref, *refs):
    extras = refs[: len(EXTRA)]
    outs = refs[len(EXTRA) + 4 : len(EXTRA) + 8]
    held = refs[len(EXTRA) + 8 : len(EXTRA) + 12]
    sems_in, sems_out = refs[len(EXTRA) + 12 :]
    moved = moved_ref[pos_ref[0]]

    def move(at, stage):
        to = pl.ds(pl.multiple_of((NB - moved + at) * BLK, BLK), BLK)
        mid = pl.ds(at * BLK, BLK)
        if at < EARLY:
            big, rows = early_ref, pl.ds(at * BLK, BLK)
        elif at < FULL:
            big, rows = main_ref, pl.ds((at - EARLY) * BLK, BLK)
        else:
            big, rows = extras[at - FULL], pl.ds(0, BLK)
        small, lines, column = (small_ref, rows, 0) if at < EARLY else (big, rows, 2 * WIDE)
        sources = (
            big.at[rows, pl.ds(0, WIDE)],
            big.at[rows, pl.ds(WIDE, WIDE)],
            small.at[lines, pl.ds(column, HD)],
            small.at[lines, pl.ds(column + HD, HD)],
        )
        for slot, source in enumerate(sources):
            come = (source, held[slot].at[mid, :], sems_in.at[4 * at + slot])
            leave = (held[slot].at[mid, :], outs[slot].at[to, :], sems_out.at[4 * at + slot])
            if stage == 0:
                pltpu.make_async_copy(*come).start()
            elif stage == 1:
                pltpu.make_async_copy(*come).wait()
                pltpu.make_async_copy(*leave).start()
            else:
                pltpu.make_async_copy(*leave).wait()

    for stage in range(3):
        for at in range(NB - 1):
            pl.when(at < moved)(functools.partial(move, at, stage))


def place(position, moved, arrived, outs):
    anywhere = pl.BlockSpec(memory_space=pl.ANY)
    return pl.pallas_call(
        place_kernel,
        grid_spec=pltpu.PrefetchScalarGridSpec(
            num_scalar_prefetch=2,
            grid=(1,),
            in_specs=[anywhere] * (len(arrived) + 4),
            out_specs=[anywhere] * 4,
            scratch_shapes=[pltpu.VMEM((ROWS - BLK, result.shape[1]), jnp.bfloat16) for result in RESULTS]
            + [pltpu.SemaphoreType.DMA((4 * (NB - 1),))] * 2,
        ),
        out_shape=RESULTS,
        input_output_aliases={2 + len(arrived) + i: i for i in range(4)},
        compiler_params=pltpu.CompilerParams(vmem_limit_bytes=8 * 1024 * 1024),
        cost_estimate=pl.CostEstimate(flops=0, bytes_accessed=2 * ROWS * WIDE * 4, transcendentals=0),
        name="place_parcels",
    )(position, moved, *arrived, *outs)


def route_kernel(pos_ref, moved_ref, after_ref, main_ref, small_ref, out_ref, main_out, small_out):
    del after_ref, main_ref, small_ref, main_out, small_out
    out_ref[0] = route_of(pos_ref[0], moved_ref)


def route(position, moved, after, main, small):
    scalar = pl.BlockSpec(memory_space=pltpu.SMEM)
    anywhere = pl.BlockSpec(memory_space=pl.ANY)
    index, main, small = pl.pallas_call(
        route_kernel,
        in_specs=[scalar, scalar, anywhere, anywhere, anywhere],
        out_specs=[scalar, anywhere, anywhere],
        out_shape=[jax.ShapeDtypeStruct((1,), jnp.int32)] + PARCELS[:2],
        input_output_aliases={3: 1, 4: 2},
        compiler_params=pltpu.CompilerParams(vmem_limit_bytes=VMEM_BYTES),
        name="route",
    )(position, moved, after, main, small)
    return index[0], main, small


def straight_route(count, swap, *extras):
    return (*[lax.ppermute(x, "dp", swap) for x in extras[:count]], *extras[count:])


def relay_route(step, side, replicas, fifth, sixth):
    half = replicas // 2
    bit = 1 << (step.bit_length() - 1)
    heavy = [r for r in range(replicas) if bool(r % LANES & bit) == bool(side)]
    halfway = lax.ppermute(sixth, "dp", [(r, (r + half) % replicas ^ step) for r in heavy])
    fifth = lax.ppermute(fifth, "dp", [(r, (r + half) % replicas) for r in heavy])
    return fifth, lax.ppermute(halfway, "dp", [(r, r ^ step) for r in range(replicas)])


def local(queries, key_rows, value_rows, out_grads, block_docs, moved_blocks):
    replicas = lax.axis_size("dp")
    swap = [(i, (i + replicas // 2) % replicas) for i in range(replicas)]
    position = lax.axis_index("dp").astype(jnp.int32).reshape(1)
    block_docs = block_docs.T
    early, dk0, dv0 = first_blocks(position, block_docs, queries, key_rows, value_rows, out_grads)
    arrived = [lax.ppermute(early, "dp", swap)]
    done = rest_blocks(position, block_docs, moved_blocks, queries, key_rows, value_rows, out_grads, early, dk0, dv0)
    (main, small, *extras), outs = done[: len(PARCELS)], done[len(PARCELS) :]
    index, main, small = route(position, moved_blocks, arrived[0], main, small)
    arrived += [lax.ppermute(main, "dp", swap), lax.ppermute(small, "dp", swap)]
    routes = [functools.partial(straight_route, count, swap) for count in range(len(EXTRA) + 1)]
    routes += [functools.partial(relay_route, step, side, replicas) for step in range(1, LANES) for side in range(2)]
    arrived += lax.switch(index, routes, *extras)
    return tuple(place(position, moved_blocks, arrived, outs))


def solution(mesh):
    placed = (P("dp", "head"), P("dp", "head"), P("dp", "head"), P("dp", "head"), P(), P())
    return jax.shard_map(
        local,
        mesh=mesh,
        in_specs=placed,
        out_specs=(P("dp", "head"), P("dp", "head"), P("dp", "head"), P("dp", "head")),
        check_vma=False,
    )
```

```python
import functools
import math

import jax
import jax.numpy as jnp
from jax import lax
from jax.experimental import pallas as pl
from jax.experimental.pallas import tpu as pltpu
from jax.sharding import PartitionSpec as P

NB = 8
BLK = 128
HQ = 8
HD = 128
WIDE = HQ * HD
ROWS = NB * BLK
GROUPS = {1: 4, 2: 4, 3: 2, 4: 2, 5: 2, 6: 2, 7: 2}
EARLY_GROUPS = {1: 8, 2: 4}
FACTOR = 1.0 / math.sqrt(HD)
LOG_FACTOR = FACTOR * math.log2(math.e)
VMEM_BYTES = 63 * 1024 * 1024


def dot(a, b, contract):
    return lax.dot_general(a, b, ((contract[:1], contract[1:]), ((), ())), preferred_element_type=jnp.float32)


def block_range(position, block, docs_ref):
    document = docs_ref[block, position]
    same = jnp.int32(0)
    for other in range(NB):
        hit = (docs_ref[other, position] == document) & (other <= block)
        same = same + jnp.where(hit, 1, 0)
    return same


def stacked(ref, head, group):
    columns = [pl.ds(pl.multiple_of((head + g) * HD, HD), HD) for g in range(group)]
    return jnp.concatenate([ref[:, at] for at in columns], axis=0)


def attend_block(blocks, group, begin, refs, write):
    q_ref, g_ref, k_ref, v_ref, kt_ref, vt_ref, dk_ref, dv_ref = refs
    width = blocks * BLK
    columns = group * BLK
    span = pl.ds(begin, width)

    def heads(turn, _):
        head = turn * group
        query = stacked(q_ref, head, group)
        grad = stacked(g_ref, head, group)
        key_place = lax.broadcasted_iota(jnp.int32, (BLK, columns), 0)
        query_place = lax.rem(lax.broadcasted_iota(jnp.int32, (BLK, columns), 1), BLK)
        scores = dot(k_ref[span, :], query, (1, 1))
        last = jnp.where(key_place <= query_place, scores[width - BLK :], -jnp.inf)
        scores = last if blocks == 1 else jnp.concatenate([scores[: width - BLK], last], axis=0)
        highest = jnp.max(scores, axis=0, keepdims=True)
        weights = jnp.exp2((scores - highest) * LOG_FACTOR)
        probs = weights * (1.0 / jnp.sum(weights, axis=0, keepdims=True))
        probs_low = probs.astype(jnp.bfloat16)
        dprobs = dot(v_ref[span, :], grad, (1, 1))
        centre = jnp.sum(probs * dprobs, axis=0, keepdims=True)
        dscores = (probs * (dprobs - centre)).astype(jnp.bfloat16)
        attended = dot(vt_ref[:, span], probs_low, (1, 0)).T.astype(jnp.bfloat16)
        query_grad = (dot(kt_ref[:, span], dscores, (1, 0)) * FACTOR).T.astype(jnp.bfloat16)
        for g in range(group):
            write(head + g, attended[g * BLK : (g + 1) * BLK], query_grad[g * BLK : (g + 1) * BLK])
        dk_ref[span, :] += dot(dscores, query, (1, 0))
        dv_ref[span, :] += dot(probs_low, grad, (1, 0))
        return 0

    lax.fori_loop(0, HQ // group, heads, 0)


def dispatch(block, groups, same, refs, write):
    for blocks, group in groups.items():

        @pl.when(same == blocks)
        def _(blocks=blocks, group=group):
            begin = pl.multiple_of((block + 1 - blocks) * BLK, BLK)
            attend_block(blocks, group, begin, refs, write)


EARLY = 2
LATE = 4
CUT = BLK // 2


def first_kernel(pos_ref, docs_ref, q_ref, g_ref, k_ref, v_ref, send_ref, dk_out, dv_out, kt, vt):
    block = pl.program_id(0)

    @pl.when(block == 0)
    def _():
        kt[...] = k_ref[...].T
        vt[...] = v_ref[...].T
        dk_out[...] = jnp.zeros_like(dk_out)
        dv_out[...] = jnp.zeros_like(dv_out)

    def write(head, attended, query_grad):
        send_ref[:, pl.ds(pl.multiple_of(head * HD, HD), HD)] = attended
        send_ref[:, pl.ds(pl.multiple_of(WIDE + head * HD, HD), HD)] = query_grad

    same = block_range(pos_ref[0], block, docs_ref)
    dispatch(block, EARLY_GROUPS, same, (q_ref, g_ref, k_ref, v_ref, kt, vt, dk_out, dv_out), write)


def first_blocks(position, docs, q, k, v, g):
    whole = lambda rows, columns: pl.BlockSpec((rows, columns), lambda i, *_: (0, 0))
    row = lambda columns: pl.BlockSpec((BLK, columns), lambda i, *_: (i, 0))
    rows = EARLY * BLK
    return pl.pallas_call(
        first_kernel,
        grid_spec=pltpu.PrefetchScalarGridSpec(
            num_scalar_prefetch=2,
            grid=(EARLY,),
            in_specs=[row(WIDE), row(WIDE), whole(rows, HD), whole(rows, HD)],
            out_specs=[row(2 * WIDE), whole(rows, HD), whole(rows, HD)],
            scratch_shapes=[pltpu.VMEM((HD, rows), jnp.bfloat16)] * 2,
        ),
        out_shape=[
            jax.ShapeDtypeStruct((rows, 2 * WIDE), jnp.bfloat16),
            jax.ShapeDtypeStruct((rows, HD), jnp.float32),
            jax.ShapeDtypeStruct((rows, HD), jnp.float32),
        ],
        compiler_params=pltpu.CompilerParams(vmem_limit_bytes=VMEM_BYTES),
        cost_estimate=pl.CostEstimate(flops=2 * 18 * HQ * BLK * BLK * HD, bytes_accessed=8 * BLK * WIDE * 2, transcendentals=0),
        name="first_blocks",
    )(position, docs, q, g, k, v)


def rest_kernel(pos_ref, docs_ref, moved_ref, q_ref, g_ref, k_ref, v_ref, early_ref, dk0_ref, dv0_ref, *rest):
    parcels = rest[: len(PARCELS)]
    att_ref, dq_ref, dk_fin, dv_fin, kt, vt, dk_ref, dv_ref = rest[len(PARCELS) :]
    step = pl.program_id(0)
    block = step + 1
    position = pos_ref[0]
    moved = moved_ref[position]

    @pl.when(step == 0)
    def _():
        kt[...] = k_ref[...].T
        vt[...] = v_ref[...].T
        dk_ref[...] = jnp.zeros_like(dk_ref)
        dv_ref[...] = jnp.zeros_like(dv_ref)
        dk_ref[: EARLY * BLK] = dk0_ref[...]
        dv_ref[: EARLY * BLK] = dv0_ref[...]
        att_ref[...] = early_ref[:, :WIDE]
        dq_ref[...] = early_ref[:, WIDE:]

    def write(head, attended, query_grad):
        here = pl.ds(pl.multiple_of(head * HD, HD), HD)
        att_ref[:, here] = attended
        dq_ref[:, here] = query_grad

    @pl.when(step > 0)
    def _():
        same = block_range(position, block, docs_ref)
        dispatch(block, GROUPS, same, (q_ref, g_ref, k_ref, v_ref, kt, vt, dk_ref, dv_ref), write)

    for at in range(EARLY, NB - 1):

        @pl.when((block == at) & (at < moved))
        def _(at=at):
            for parcel, row, line, rows in copies_of(at):
                parcels[parcel][row : row + rows, :WIDE] = att_ref[line : line + rows]
                parcels[parcel][row : row + rows, WIDE : 2 * WIDE] = dq_ref[line : line + rows]

    @pl.when(step == NB - 2)
    def _():
        for at in range(NB):
            rows = slice(at * BLK, (at + 1) * BLK)
            dk = (dk_ref[rows] * FACTOR).astype(jnp.bfloat16)
            dv = dv_ref[rows].astype(jnp.bfloat16)
            if at < NB - 1:
                if at < EARLY:
                    for turn in range(TURNS):
                        lines = slice(turn * FOLD, (turn + 1) * FOLD)
                        column = (at * TURNS + turn) * 2 * HD
                        parcels[0][BLK:, column : column + HD] = dk[lines]
                        parcels[0][BLK:, column + HD : column + 2 * HD] = dv[lines]
                else:
                    for parcel, row, line, count in copies_of(at):
                        parcels[parcel][row : row + count, 2 * WIDE : 2 * WIDE + HD] = dk[line : line + count]
                        parcels[parcel][row : row + count, 2 * WIDE + HD :] = dv[line : line + count]
            if at > 0:

                @pl.when(at >= moved)
                def _():
                    to = pl.ds(pl.multiple_of((at - moved) * BLK, BLK), BLK)
                    dk_fin[to, :] = dk
                    dv_fin[to, :] = dv


FOLD = EARLY * BLK * HD // WIDE
TURNS = BLK // FOLD
PARCEL_ROWS = (BLK + FOLD, BLK, BLK + CUT, 2 * BLK - CUT, 2 * BLK, BLK)
PARCELS = [jax.ShapeDtypeStruct((rows, 2 * WIDE + 2 * HD), jnp.bfloat16) for rows in PARCEL_ROWS]
SECOND, THIRD, OWN, RELAYED, PAIR, LAST = range(len(PARCELS))


def copies_of(at, relayed=None):
    if at < LATE:
        return [(SECOND if at == EARLY else THIRD, 0, 0, BLK)]
    cut = {
        LATE: [(OWN, 0, 0, BLK)],
        LATE + 1: [(OWN, BLK, 0, CUT), (RELAYED, 0, CUT, BLK - CUT)],
        LATE + 2: [(RELAYED, BLK - CUT, 0, BLK)],
    }[at]
    plain = [(LAST, 0, 0, BLK)] if at == LATE + 2 else [(PAIR, (at - LATE) * BLK, 0, BLK)]
    return cut + plain if relayed is None else cut if relayed else plain


RESULTS = [jax.ShapeDtypeStruct((ROWS, columns), jnp.bfloat16) for columns in (WIDE, WIDE, HD, HD)]


def rest_blocks(position, docs, moved, q, k, v, g, early, dk0, dv0):
    def stay(i, pos, docs, moved):
        return (jnp.maximum(i + 1 - moved[pos[0]], 0), 0)

    whole = lambda rows, columns: pl.BlockSpec((rows, columns), lambda i, *_: (0, 0))
    row = pl.BlockSpec((BLK, WIDE), lambda i, *_: (jnp.maximum(i + 1, EARLY), 0))
    early_row = pl.BlockSpec((BLK, 2 * WIDE), lambda i, *_: (1, 0))
    return pl.pallas_call(
        rest_kernel,
        grid_spec=pltpu.PrefetchScalarGridSpec(
            num_scalar_prefetch=3,
            grid=(NB - 1,),
            in_specs=[row, row, whole(ROWS, HD), whole(ROWS, HD), early_row, whole(EARLY * BLK, HD), whole(EARLY * BLK, HD)],
            out_specs=[whole(*parcel.shape) for parcel in PARCELS]
            + [
                pl.BlockSpec((BLK, WIDE), stay),
                pl.BlockSpec((BLK, WIDE), stay),
                whole(ROWS, HD),
                whole(ROWS, HD),
            ],
            scratch_shapes=[pltpu.VMEM((HD, ROWS), jnp.bfloat16)] * 2 + [pltpu.VMEM((ROWS, HD), jnp.float32)] * 2,
        ),
        out_shape=[pltpu.HBM(parcel.shape, parcel.dtype) for parcel in PARCELS] + RESULTS,
        compiler_params=pltpu.CompilerParams(vmem_limit_bytes=VMEM_BYTES),
        cost_estimate=pl.CostEstimate(flops=2 * 6 * HQ * BLK * BLK * HD * 20, bytes_accessed=8 * ROWS * WIDE, transcendentals=0),
        name="rest_blocks",
    )(position, docs, moved, q, g, k, v, early, dk0, dv0)


LANES = 8
STEPS = (1, 7, 3, 2, 6, 5)
PLAIN = NB - LATE


def route_of(position, moved_ref):
    lane = lax.rem(position, LANES)
    base = lax.rem(position, 2 * LANES) - lane
    load = [moved_ref[base + z] for z in range(LANES)]
    free = [jnp.int32(1)] * LANES
    index = jnp.maximum(moved_ref[position], LATE) - LATE
    for most in (NB - 1, NB - 2):
        for turn, step in enumerate(STEPS):
            for z in range(LANES):
                mate = z ^ step
                met = jnp.where((load[z] == most) & (load[mate] <= LATE), free[z] * free[mate], 0)
                free[z], free[mate] = free[z] - met, free[mate] - met
                side = 1 if z & top_bit(step) else 0
                mine = (met == 1) & ((lane == z) | (lane == mate))
                index = jnp.where(mine, PLAIN + turn * 2 + side, index)
    return index


def top_bit(step):
    return 1 << (step.bit_length() - 1)


def place_kernel(pos_ref, moved_ref, index_ref, early_ref, *refs):
    count = len(PARCELS)
    parcels = refs[:count]
    outs = refs[count + 4 : count + 8]
    held = refs[count + 8 : count + 12]
    sems_in, sems_out = refs[count + 12 :]
    moved = moved_ref[pos_ref[0]]
    cut = (index_ref[0] >= PLAIN) | (index_ref[0] == 1)

    def sources(at, relayed):
        if at >= EARLY:
            return [
                [(parcels[p].at[pl.ds(row, rows), pl.ds(c, w)], line, rows) for p, row, line, rows in copies_of(at, relayed)]
                for c, w in ((0, WIDE), (WIDE, WIDE), (2 * WIDE, HD), (2 * WIDE + HD, HD))
            ]
        big = early_ref.at[pl.ds(at * BLK, BLK)]
        pieces = [[(big.at[:, pl.ds(c, WIDE)], 0, BLK)] for c in (0, WIDE)]
        for shift in (0, HD):
            columns = [(at * TURNS + turn) * 2 * HD + shift for turn in range(TURNS)]
            pieces.append([(parcels[0].at[pl.ds(BLK, FOLD), pl.ds(c, HD)], turn * FOLD, FOLD) for turn, c in enumerate(columns)])
        return pieces

    def move(at, stage, relayed):
        to = pl.ds(pl.multiple_of((NB - moved + at) * BLK, BLK), BLK)
        for slot, pieces in enumerate(sources(at, relayed)):
            mid = held[slot].at[pl.ds(at * BLK, BLK)]
            for turn, (source, row, rows) in enumerate(pieces):
                come = (source, mid.at[pl.ds(row, rows)], sems_in.at[at, slot, turn])
                if stage == 0:
                    pltpu.make_async_copy(*come).start()
                elif stage == 1:
                    pltpu.make_async_copy(*come).wait()
            if stage == 1:
                pltpu.make_async_copy(mid, outs[slot].at[to], sems_out.at[at, slot]).start()
            elif stage == 2:
                pltpu.make_async_copy(mid, outs[slot].at[to], sems_out.at[at, slot]).wait()

    for stage in range(3):
        for at in range(NB - 1):
            if at >= LATE:
                pl.when((at < moved) & cut)(functools.partial(move, at, stage, True))
                pl.when((at < moved) & jnp.logical_not(cut))(functools.partial(move, at, stage, False))
            else:
                pl.when(at < moved)(functools.partial(move, at, stage, False))


def place(position, moved, index, arrived, outs):
    anywhere = pl.BlockSpec(memory_space=pl.ANY)
    return pl.pallas_call(
        place_kernel,
        grid_spec=pltpu.PrefetchScalarGridSpec(
            num_scalar_prefetch=3,
            grid=(1,),
            in_specs=[anywhere] * (len(arrived) + 4),
            out_specs=[anywhere] * 4,
            scratch_shapes=[pltpu.VMEM((ROWS - BLK, result.shape[1]), jnp.bfloat16) for result in RESULTS]
            + [pltpu.SemaphoreType.DMA((NB - 1, 4, TURNS)), pltpu.SemaphoreType.DMA((NB - 1, 4))],
        ),
        out_shape=RESULTS,
        input_output_aliases={3 + len(arrived) + i: i for i in range(4)},
        compiler_params=pltpu.CompilerParams(vmem_limit_bytes=8 * 1024 * 1024),
        cost_estimate=pl.CostEstimate(flops=0, bytes_accessed=2 * ROWS * WIDE * 4, transcendentals=0),
        name="place_parcels",
    )(position, moved, index, *arrived, *outs)


def blank_kernel(out_ref):
    del out_ref


def blank(like):
    return pl.pallas_call(
        blank_kernel,
        out_specs=pl.BlockSpec(memory_space=pl.ANY),
        out_shape=jax.ShapeDtypeStruct(like.shape, like.dtype),
        compiler_params=pltpu.CompilerParams(vmem_limit_bytes=1024 * 1024),
        name="blank",
    )()


def route_kernel(pos_ref, moved_ref, after_ref, out_ref):
    del after_ref
    out_ref[0] = route_of(pos_ref[0], moved_ref)


def route(position, moved, after):
    scalar = pl.BlockSpec(memory_space=pltpu.SMEM)
    return pl.pallas_call(
        route_kernel,
        in_specs=[scalar, scalar, pl.BlockSpec(memory_space=pl.ANY)],
        out_specs=scalar,
        out_shape=jax.ShapeDtypeStruct((1,), jnp.int32),
        compiler_params=pltpu.CompilerParams(vmem_limit_bytes=VMEM_BYTES),
        name="route",
    )(position, moved, after)


def straight_route(count, swap, own, relayed, pair, last):
    send = lambda use, x: lax.ppermute(x, "dp", swap) if use else blank(x)
    return send(count == 1, own), blank(relayed), send(count > 1, pair), send(count > 2, last)


def relay_route(step, side, swap, own, relayed, pair, last):
    heavy = [r for r, _ in swap if bool(r & top_bit(step)) == bool(side)]
    halfway = lax.ppermute(relayed, "dp", [(r, swap[r][1] ^ step) for r in heavy])
    own = lax.ppermute(own, "dp", [(r, swap[r][1]) for r in heavy])
    return own, lax.ppermute(halfway, "dp", [(r ^ step, r) for r in heavy]), blank(pair), blank(last)


def local(queries, key_rows, value_rows, out_grads, block_docs, moved_blocks):
    replicas = lax.axis_size("dp")
    swap = [(i, (i + replicas // 2) % replicas) for i in range(replicas)]
    position = lax.axis_index("dp").astype(jnp.int32).reshape(1)
    block_docs = block_docs.T
    early, dk0, dv0 = first_blocks(position, block_docs, queries, key_rows, value_rows, out_grads)
    arrived = [lax.ppermute(early, "dp", swap)]
    done = rest_blocks(position, block_docs, moved_blocks, queries, key_rows, value_rows, out_grads, early, dk0, dv0)
    parcels, outs = done[: len(PARCELS)], done[len(PARCELS) :]
    arrived += [lax.ppermute(parcels[at], "dp", swap) for at in (SECOND, THIRD)]
    index = route(position, moved_blocks, dk0)
    routes = [functools.partial(straight_route, count, swap) for count in range(PLAIN)]
    routes += [functools.partial(relay_route, step, side, swap) for step in STEPS for side in range(2)]
    arrived += lax.switch(index[0], routes, *parcels[OWN:])
    return tuple(place(position, moved_blocks, index, arrived, outs))


def solution(mesh):
    placed = (P("dp", "head"), P("dp", "head"), P("dp", "head"), P("dp", "head"), P(), P())
    return jax.shard_map(
        local,
        mesh=mesh,
        in_specs=placed,
        out_specs=(P("dp", "head"), P("dp", "head"), P("dp", "head"), P("dp", "head")),
        check_vma=False,
    )
```

```python
import functools
import math

import jax
import jax.numpy as jnp
from jax import lax
from jax.experimental import pallas as pl
from jax.experimental.pallas import tpu as pltpu
from jax.sharding import PartitionSpec as P

NB = 8
BLK = 128
HQ = 8
HD = 128
WIDE = HQ * HD
ROWS = NB * BLK
GROUPS = {1: 8, 2: 8, 3: 8, 4: 4, 5: 4, 6: 4, 7: 4}
EARLY_GROUPS = {1: 8, 2: 4}
FACTOR = 1.0 / math.sqrt(HD)
LOG_FACTOR = FACTOR * math.log2(math.e)
VMEM_BYTES = 58 * 1024 * 1024


def dot(a, b, contract):
    return lax.dot_general(a, b, ((contract[:1], contract[1:]), ((), ())), preferred_element_type=jnp.float32)


def block_range(position, block, docs_ref):
    document = docs_ref[block, position]
    same = jnp.int32(0)
    for other in range(NB):
        hit = (docs_ref[other, position] == document) & (other <= block)
        same = same + jnp.where(hit, 1, 0)
    return same


def stacked(ref, head, group):
    columns = [pl.ds(pl.multiple_of((head + g) * HD, HD), HD) for g in range(group)]
    return jnp.concatenate([ref[:, at] for at in columns], axis=0)


def attend_block(blocks, group, begin, refs, write):
    q_ref, g_ref, k_ref, v_ref, kt_ref, vt_ref, dk_ref, dv_ref = refs
    width = blocks * BLK
    columns = group * BLK
    span = pl.ds(begin, width)

    def heads(turn, _):
        head = turn * group
        query = stacked(q_ref, head, group)
        grad = stacked(g_ref, head, group)
        key_place = lax.broadcasted_iota(jnp.int32, (BLK, columns), 0)
        query_place = lax.rem(lax.broadcasted_iota(jnp.int32, (BLK, columns), 1), BLK)
        scores = dot(k_ref[span, :], query, (1, 1))
        last = jnp.where(key_place <= query_place, scores[width - BLK :], -jnp.inf)
        scores = last if blocks == 1 else jnp.concatenate([scores[: width - BLK], last], axis=0)
        highest = jnp.max(scores, axis=0, keepdims=True)
        weights = jnp.exp2((scores - highest) * LOG_FACTOR)
        probs = weights * (1.0 / jnp.sum(weights, axis=0, keepdims=True))
        probs_low = probs.astype(jnp.bfloat16)
        dprobs = dot(v_ref[span, :], grad, (1, 1))
        centre = jnp.sum(probs * dprobs, axis=0, keepdims=True)
        dscores = (probs * (dprobs - centre)).astype(jnp.bfloat16)
        attended = dot(vt_ref[:, span], probs_low, (1, 0)).T.astype(jnp.bfloat16)
        query_grad = (dot(kt_ref[:, span], dscores, (1, 0)) * FACTOR).T.astype(jnp.bfloat16)
        for g in range(group):
            write(head + g, attended[g * BLK : (g + 1) * BLK], query_grad[g * BLK : (g + 1) * BLK])
        dk_ref[span, :] += dot(dscores, query, (1, 0))
        dv_ref[span, :] += dot(probs_low, grad, (1, 0))
        return 0

    lax.fori_loop(0, HQ // group, heads, 0)


def dispatch(block, groups, same, refs, write):
    for blocks, group in groups.items():

        @pl.when(same == blocks)
        def _(blocks=blocks, group=group):
            begin = pl.multiple_of((block + 1 - blocks) * BLK, BLK)
            attend_block(blocks, group, begin, refs, write)


EARLY = 2
LATE = 4
CUT = BLK // 2


def first_kernel(pos_in, docs_in, q_ref, g_ref, k_ref, v_ref, send_ref, dk_out, dv_out, kt, vt, pos_ref, docs_ref, sems):
    block = pl.program_id(0)
    reads = [pltpu.make_async_copy(pos_in, pos_ref, sems.at[0]), pltpu.make_async_copy(docs_in, docs_ref, sems.at[1])]

    @pl.when(block == 0)
    def _():
        for read in reads:
            read.start()
        kt[...] = k_ref[...].T
        vt[...] = v_ref[...].T
        dk_out[...] = jnp.zeros_like(dk_out)
        dv_out[...] = jnp.zeros_like(dv_out)

    def write(head, attended, query_grad):
        send_ref[:, pl.ds(pl.multiple_of(head * HD, HD), HD)] = attended
        send_ref[:, pl.ds(pl.multiple_of(WIDE + head * HD, HD), HD)] = query_grad

    refs = (q_ref, g_ref, k_ref, v_ref, kt, vt, dk_out, dv_out)

    @pl.when(block == 0)
    def _():
        attend_block(1, EARLY_GROUPS[1], 0, refs, write)
        for read in reads:
            read.wait()

    @pl.when(block > 0)
    def _():
        dispatch(block, EARLY_GROUPS, block_range(pos_ref[0], block, docs_ref), refs, write)


def first_blocks(position, docs, q, k, v, g):
    whole = lambda rows, columns: pl.BlockSpec((rows, columns), lambda i, *_: (0, 0))
    row = lambda columns: pl.BlockSpec((BLK, columns), lambda i, *_: (i, 0))
    rows = EARLY * BLK
    return pl.pallas_call(
        first_kernel,
        grid=(EARLY,),
        in_specs=[pl.BlockSpec(memory_space=pl.ANY)] * 2 + [row(WIDE), row(WIDE), whole(rows, HD), whole(rows, HD)],
        out_specs=[row(2 * WIDE), whole(rows, HD), whole(rows, HD)],
        scratch_shapes=[pltpu.VMEM((HD, rows), jnp.bfloat16)] * 2
        + [pltpu.SMEM(position.shape, jnp.int32), pltpu.SMEM(docs.shape, jnp.int32), pltpu.SemaphoreType.DMA((2,))],
        out_shape=[
            jax.ShapeDtypeStruct((rows, 2 * WIDE), jnp.bfloat16),
            jax.ShapeDtypeStruct((rows, HD), jnp.float32),
            jax.ShapeDtypeStruct((rows, HD), jnp.float32),
        ],
        compiler_params=pltpu.CompilerParams(vmem_limit_bytes=VMEM_BYTES),
        cost_estimate=pl.CostEstimate(flops=2 * 18 * HQ * BLK * BLK * HD, bytes_accessed=8 * BLK * WIDE * 2, transcendentals=0),
        name="first_blocks",
    )(position, docs, q, g, k, v)


def rest_kernel(pos_ref, docs_ref, moved_ref, q_ref, g_ref, k_ref, v_ref, early_ref, dk0_ref, dv0_ref, *rest):
    route_ref, *parcels = rest[: 1 + len(PARCELS)]
    att_ref, dq_ref, dk_fin, dv_fin, kt, vt, dk_ref, dv_ref = rest[1 + len(PARCELS) :]
    step = pl.program_id(0)
    block = step + 1
    position = pos_ref[0]
    moved = moved_ref[position]

    @pl.when(step == 0)
    def _():
        route_ref[0] = route_of(position, moved_ref)
        route_ref[1] = moved
        kt[...] = k_ref[...].T
        vt[...] = v_ref[...].T
        dk_ref[...] = jnp.zeros_like(dk_ref)
        dv_ref[...] = jnp.zeros_like(dv_ref)
        dk_ref[: EARLY * BLK] = dk0_ref[...]
        dv_ref[: EARLY * BLK] = dv0_ref[...]
        att_ref[...] = early_ref[:, :WIDE]
        dq_ref[...] = early_ref[:, WIDE:]

    def write(head, attended, query_grad):
        here = pl.ds(pl.multiple_of(head * HD, HD), HD)
        att_ref[:, here] = attended
        dq_ref[:, here] = query_grad

    @pl.when(step > 0)
    def _():
        same = block_range(position, block, docs_ref)
        dispatch(block, GROUPS, same, (q_ref, g_ref, k_ref, v_ref, kt, vt, dk_ref, dv_ref), write)

    for at in range(EARLY, NB - 1):

        @pl.when((block == at) & (at < moved))
        def _(at=at):
            for parcel, row, line, rows in copies_of(at):
                parcels[parcel][row : row + rows, :WIDE] = att_ref[line : line + rows]
                parcels[parcel][row : row + rows, WIDE : 2 * WIDE] = dq_ref[line : line + rows]

    @pl.when(step == NB - 2)
    def _():
        for at in range(NB):
            rows = slice(at * BLK, (at + 1) * BLK)
            dk = (dk_ref[rows] * FACTOR).astype(jnp.bfloat16)
            dv = dv_ref[rows].astype(jnp.bfloat16)
            if at < NB - 1:
                if at < EARLY:
                    for turn in range(TURNS):
                        lines = slice(turn * FOLD, (turn + 1) * FOLD)
                        column = (at * TURNS + turn) * 2 * HD
                        parcels[0][BLK:, column : column + HD] = dk[lines]
                        parcels[0][BLK:, column + HD : column + 2 * HD] = dv[lines]
                else:
                    for parcel, row, line, count in copies_of(at):
                        parcels[parcel][row : row + count, 2 * WIDE : 2 * WIDE + HD] = dk[line : line + count]
                        parcels[parcel][row : row + count, 2 * WIDE + HD :] = dv[line : line + count]
            if at > 0:

                @pl.when(at >= moved)
                def _():
                    to = pl.ds(pl.multiple_of((at - moved) * BLK, BLK), BLK)
                    dk_fin[to, :] = dk
                    dv_fin[to, :] = dv


FOLD = EARLY * BLK * HD // WIDE
TURNS = BLK // FOLD
PARCEL_ROWS = (BLK + FOLD, BLK, BLK + CUT, 2 * BLK - CUT, 2 * BLK, BLK)
PARCELS = [jax.ShapeDtypeStruct((rows, 2 * WIDE + 2 * HD), jnp.bfloat16) for rows in PARCEL_ROWS]
SECOND, THIRD, OWN, RELAYED, PAIR, LAST = range(len(PARCELS))
RESIDENT = 1 + OWN


def copies_of(at, relayed=None):
    if at < LATE:
        return [(SECOND if at == EARLY else THIRD, 0, 0, BLK)]
    cut = {
        LATE: [(OWN, 0, 0, BLK)],
        LATE + 1: [(OWN, BLK, 0, CUT), (RELAYED, 0, CUT, BLK - CUT)],
        LATE + 2: [(RELAYED, BLK - CUT, 0, BLK)],
    }[at]
    plain = [(LAST, 0, 0, BLK)] if at == LATE + 2 else [(PAIR, (at - LATE) * BLK, 0, BLK)]
    return cut + plain if relayed is None else cut if relayed else plain


RESULTS = [jax.ShapeDtypeStruct((ROWS, columns), jnp.bfloat16) for columns in (WIDE, WIDE, HD, HD)]


def rest_blocks(position, docs, moved, q, k, v, g, early, dk0, dv0):
    def stay(i, pos, docs, moved):
        return (jnp.maximum(i + 1 - moved[pos[0]], 0), 0)

    whole = lambda rows, columns: pl.BlockSpec((rows, columns), lambda i, *_: (0, 0))
    row = pl.BlockSpec((BLK, WIDE), lambda i, *_: (jnp.maximum(i + 1, EARLY), 0))
    early_row = pl.BlockSpec((BLK, 2 * WIDE), lambda i, *_: (1, 0))
    return pl.pallas_call(
        rest_kernel,
        grid_spec=pltpu.PrefetchScalarGridSpec(
            num_scalar_prefetch=3,
            grid=(NB - 1,),
            in_specs=[row, row, whole(ROWS, HD), whole(ROWS, HD), early_row, whole(EARLY * BLK, HD), whole(EARLY * BLK, HD)],
            out_specs=[pl.BlockSpec(memory_space=pltpu.SMEM)]
            + [whole(*parcel.shape) for parcel in PARCELS]
            + [
                pl.BlockSpec((BLK, WIDE), stay),
                pl.BlockSpec((BLK, WIDE), stay),
                whole(ROWS, HD),
                whole(ROWS, HD),
            ],
            scratch_shapes=[pltpu.VMEM((HD, ROWS), jnp.bfloat16)] * 2 + [pltpu.VMEM((ROWS, HD), jnp.float32)] * 2,
        ),
        out_shape=[jax.ShapeDtypeStruct((2,), jnp.int32)] + [pltpu.HBM(x.shape, x.dtype) for x in PARCELS] + RESULTS,
        compiler_params=pltpu.CompilerParams(vmem_limit_bytes=VMEM_BYTES),
        cost_estimate=pl.CostEstimate(flops=2 * 6 * HQ * BLK * BLK * HD * 20, bytes_accessed=8 * ROWS * WIDE, transcendentals=0),
        name="rest_blocks",
    )(position, docs, moved, q, g, k, v, early, dk0, dv0)


LANES = 8
STEPS = (1, 7, 3, 2, 6, 5)
PLAIN = NB - LATE


def z_path(z, mate):
    up = (mate - z) % LANES
    if up < LANES - up:
        return sum(1 << (z + hop) % LANES for hop in range(up)), up
    return sum(1 << LANES + (z - hop) % LANES for hop in range(LANES - up)), LANES - up


def route_of(position, moved_ref):
    lane = lax.rem(position, LANES)
    base = lax.rem(position, 2 * LANES) - lane
    load = [moved_ref[base + z] for z in range(LANES)]
    free = [jnp.int32(1)] * LANES
    taken = jnp.int32(0)
    index = jnp.maximum(moved_ref[position], LATE) - LATE
    pairs = [(step, z, *z_path(z, z ^ step)) for step in STEPS for z in range(LANES)]
    for most in (NB - 1, NB - 2):
        for step, z, links, _ in sorted(pairs, key=lambda pair: pair[3]):
            mate = z ^ step
            met = jnp.where((load[z] == most) & (load[mate] <= LATE) & ((taken & links) == 0), free[z] * free[mate], 0)
            free[z], free[mate] = free[z] - met, free[mate] - met
            taken = taken + met * links
            side = 1 if z & top_bit(step) else 0
            mine = (met == 1) & ((lane == z) | (lane == mate))
            index = jnp.where(mine, PLAIN + STEPS.index(step) * 2 + side, index)
    return index


def top_bit(step):
    return 1 << (step.bit_length() - 1)


def place_kernel(route_ref, *refs):
    count = 1 + len(PARCELS)
    arrived = refs[:count]
    outs = refs[count + 4 : count + 8]
    held = refs[count + 8 : count + 8 + count - RESIDENT]
    strip, small, numbers, sems_in, sems_out = refs[count + 8 + count - RESIDENT :]
    early, parcels = arrived[0], (*arrived[1:RESIDENT], *held)

    def come(which, start):
        if which == 1 + SECOND:
            copy = pltpu.make_async_copy(arrived[which].at[pl.ds(BLK, FOLD)], strip, sems_in.at[which])
        else:
            copy = pltpu.make_async_copy(arrived[which], held[which - RESIDENT], sems_in.at[which])
        if start:
            copy.start()
        else:
            copy.wait()

    read = pltpu.make_async_copy(route_ref, numbers, sems_in.at[count])
    read.start()
    for which in (1 + OWN, 1 + RELAYED, 1 + SECOND):
        come(which, True)
    read.wait()
    route, moved = numbers[0], numbers[1]
    cut = (route >= PLAIN) | (route == 1)
    plain = jnp.logical_not(cut)
    wanted = {
        1 + PAIR: plain & (moved > LATE),
        1 + LAST: plain & (moved > LATE + 2),
    }
    for which, needed in wanted.items():
        pl.when(needed)(functools.partial(come, which, True))
    columns = ((0, WIDE), (WIDE, WIDE), (2 * WIDE, HD), (2 * WIDE + HD, HD))

    def leave(at, relayed, start):
        begin = (NB - moved + at) * BLK
        pieces = []
        if at < EARLY:
            rows = pl.ds(at * BLK, BLK)
            pieces += [(slot, early.at[rows, pl.ds(slot * WIDE, WIDE)], 0, BLK) for slot in range(2)]
            pieces += [(2 + slot, small.at[rows, pl.ds(slot * HD, HD)], 0, BLK) for slot in range(2)]
        else:
            for parcel, row, line, rows in copies_of(at, relayed):
                for slot, (column, width) in enumerate(columns):
                    pieces.append((slot, parcels[parcel].at[pl.ds(row, rows), pl.ds(column, width)], line, rows))
        for turn, (slot, source, line, rows) in enumerate(pieces):
            to = pl.ds(pl.multiple_of(begin + line, CUT), rows)
            copy = pltpu.make_async_copy(source, outs[slot].at[to], sems_out.at[at, turn])
            if start:
                copy.start()
            else:
                copy.wait()

    def each_block(blocks, start):
        for at in blocks:
            if at < LATE:
                pl.when(at < moved)(functools.partial(leave, at, None, start))
            else:
                pl.when((at < moved) & cut)(functools.partial(leave, at, True, start))
                pl.when((at < moved) & plain)(functools.partial(leave, at, False, start))

    each_block(range(EARLY, LATE), True)
    come(1 + SECOND, False)
    for turn in range(EARLY * TURNS):
        small[turn * FOLD : (turn + 1) * FOLD] = strip[:, turn * 2 * HD : (turn + 1) * 2 * HD]
    each_block(range(EARLY), True)
    for which in (1 + OWN, 1 + RELAYED):
        come(which, False)
    for which, needed in wanted.items():
        pl.when(needed)(functools.partial(come, which, False))
    each_block(range(LATE, NB - 1), True)
    each_block(range(NB - 1), False)


def place(route, arrived, outs):
    anywhere = pl.BlockSpec(memory_space=pl.ANY)
    arrived = [pltpu.with_memory_space_constraint(x, pltpu.VMEM) if at < RESIDENT else x for at, x in enumerate(arrived)]
    return pl.pallas_call(
        place_kernel,
        in_specs=[anywhere] * (1 + len(arrived) + 4),
        out_specs=[anywhere] * 4,
        scratch_shapes=[pltpu.VMEM(x.shape, x.dtype) for x in arrived[RESIDENT:]]
        + [
            pltpu.VMEM((FOLD, 2 * WIDE + 2 * HD), jnp.bfloat16),
            pltpu.VMEM((EARLY * BLK, 2 * HD), jnp.bfloat16),
            pltpu.SMEM(route.shape, route.dtype),
            pltpu.SemaphoreType.DMA((len(arrived) + 1,)),
            pltpu.SemaphoreType.DMA((NB - 1, 8)),
        ],
        out_shape=RESULTS,
        input_output_aliases={1 + len(arrived) + i: i for i in range(4)},
        compiler_params=pltpu.CompilerParams(vmem_limit_bytes=10 * 1024 * 1024),
        cost_estimate=pl.CostEstimate(flops=0, bytes_accessed=2 * ROWS * WIDE * 4, transcendentals=0),
        name="place_parcels",
    )(route, *arrived, *outs)


def blank_kernel(out_ref):
    del out_ref


def blank(like):
    return pl.pallas_call(
        blank_kernel,
        out_specs=pl.BlockSpec(memory_space=pl.ANY),
        out_shape=jax.ShapeDtypeStruct(like.shape, like.dtype),
        compiler_params=pltpu.CompilerParams(vmem_limit_bytes=1024 * 1024),
        name="blank",
    )()


def straight_route(count, swap, own, relayed, pair, last):
    send = lambda use, x: lax.ppermute(x, "dp", swap) if use else blank(x)
    return send(count == 1, own), blank(relayed), send(count > 1, pair), send(count > 2, last)


def relay_route(step, side, swap, own, relayed, pair, last):
    heavy = [r for r, _ in swap if bool(r & top_bit(step)) == bool(side)]
    halfway = lax.ppermute(relayed, "dp", [(r, swap[r][1] ^ step) for r in heavy])
    own = lax.ppermute(own, "dp", [(r, swap[r][1]) for r in heavy])
    return own, lax.ppermute(halfway, "dp", [(r ^ step, r) for r in heavy]), blank(pair), blank(last)


def local(queries, key_rows, value_rows, out_grads, block_docs, moved_blocks):
    replicas = lax.axis_size("dp")
    swap = [(i, (i + replicas // 2) % replicas) for i in range(replicas)]
    position = lax.axis_index("dp").astype(jnp.int32).reshape(1)
    block_docs = block_docs.T
    early, dk0, dv0 = first_blocks(position, block_docs, queries, key_rows, value_rows, out_grads)
    arrived = [lax.ppermute(early, "dp", swap)]
    done = rest_blocks(position, block_docs, moved_blocks, queries, key_rows, value_rows, out_grads, early, dk0, dv0)
    route, parcels, outs = done[0], done[1 : 1 + len(PARCELS)], done[1 + len(PARCELS) :]
    arrived += [lax.ppermute(parcels[at], "dp", swap) for at in (SECOND, THIRD)]
    routes = [functools.partial(straight_route, count, swap) for count in range(PLAIN)]
    routes += [functools.partial(relay_route, step, side, swap) for step in STEPS for side in range(2)]
    arrived += lax.switch(route[0], routes, *parcels[OWN:])
    return tuple(place(route, arrived, outs))


def solution(mesh):
    placed = (P("dp", "head"), P("dp", "head"), P("dp", "head"), P("dp", "head"), P(), P())
    return jax.shard_map(
        local,
        mesh=mesh,
        in_specs=placed,
        out_specs=(P("dp", "head"), P("dp", "head"), P("dp", "head"), P("dp", "head")),
        check_vma=False,
    )
```

```python
import functools
import math

import jax
import jax.numpy as jnp
from jax import lax
from jax.experimental import pallas as pl
from jax.experimental.pallas import tpu as pltpu
from jax.sharding import PartitionSpec as P

NB = 8
BLK = 128
HQ = 8
HD = 128
WIDE = HQ * HD
ROWS = NB * BLK
GROUPS = {1: 8, 2: 8, 3: 8, 4: 4, 5: 4, 6: 4, 7: 4}
EARLY_GROUPS = {1: 8, 2: 8}
FACTOR = 1.0 / math.sqrt(HD)
LOG_FACTOR = FACTOR * math.log2(math.e)
VMEM_BYTES = 58 * 1024 * 1024


def dot(a, b, contract):
    return lax.dot_general(a, b, ((contract[:1], contract[1:]), ((), ())), preferred_element_type=jnp.float32)


def block_range(position, block, docs_ref):
    document = docs_ref[block, position]
    same = jnp.int32(0)
    for other in range(NB):
        hit = (docs_ref[other, position] == document) & (other <= block)
        same = same + jnp.where(hit, 1, 0)
    return same


def stacked(ref, head, group):
    columns = [pl.ds(pl.multiple_of((head + g) * HD, HD), HD) for g in range(group)]
    return jnp.concatenate([ref[:, at] for at in columns], axis=0)


def attend_block(blocks, group, begin, refs, write):
    q_ref, g_ref, k_ref, v_ref, kt_ref, vt_ref, dk_ref, dv_ref = refs
    width = blocks * BLK
    columns = group * BLK
    span = pl.ds(begin, width)

    def heads(turn, _):
        head = turn * group
        query = stacked(q_ref, head, group)
        grad = stacked(g_ref, head, group)
        key_place = lax.broadcasted_iota(jnp.int32, (BLK, columns), 0)
        query_place = lax.rem(lax.broadcasted_iota(jnp.int32, (BLK, columns), 1), BLK)
        scores = dot(k_ref[span, :], query, (1, 1))
        last = jnp.where(key_place <= query_place, scores[width - BLK :], -jnp.inf)
        scores = last if blocks == 1 else jnp.concatenate([scores[: width - BLK], last], axis=0)
        highest = jnp.max(scores, axis=0, keepdims=True)
        weights = jnp.exp2((scores - highest) * LOG_FACTOR)
        probs = weights * (1.0 / jnp.sum(weights, axis=0, keepdims=True))
        probs_low = probs.astype(jnp.bfloat16)
        dprobs = dot(v_ref[span, :], grad, (1, 1))
        centre = jnp.sum(probs * dprobs, axis=0, keepdims=True)
        dscores = (probs * (dprobs - centre)).astype(jnp.bfloat16)
        attended = dot(vt_ref[:, span], probs_low, (1, 0)).T.astype(jnp.bfloat16)
        query_grad = (dot(kt_ref[:, span], dscores, (1, 0)) * FACTOR).T.astype(jnp.bfloat16)
        for g in range(group):
            write(head + g, attended[g * BLK : (g + 1) * BLK], query_grad[g * BLK : (g + 1) * BLK])
        dk_ref[span, :] += dot(dscores, query, (1, 0))
        dv_ref[span, :] += dot(probs_low, grad, (1, 0))
        return 0

    lax.fori_loop(0, HQ // group, heads, 0)


def dispatch(block, groups, same, refs, write):
    for blocks, group in groups.items():

        @pl.when(same == blocks)
        def _(blocks=blocks, group=group):
            begin = pl.multiple_of((block + 1 - blocks) * BLK, BLK)
            attend_block(blocks, group, begin, refs, write)


EARLY = 2
LATE = 4
CUT = BLK // 2


def first_kernel(pos_in, docs_in, q_ref, g_ref, k_ref, v_ref, send_ref, dk_out, dv_out, kt, vt, pos_ref, docs_ref, sems):
    block = pl.program_id(0)
    reads = [pltpu.make_async_copy(pos_in, pos_ref, sems.at[0]), pltpu.make_async_copy(docs_in, docs_ref, sems.at[1])]

    @pl.when(block == 0)
    def _():
        for read in reads:
            read.start()
        kt[...] = k_ref[...].T
        vt[...] = v_ref[...].T
        dk_out[...] = jnp.zeros_like(dk_out)
        dv_out[...] = jnp.zeros_like(dv_out)

    def write(head, attended, query_grad):
        send_ref[:, pl.ds(pl.multiple_of(head * HD, HD), HD)] = attended
        send_ref[:, pl.ds(pl.multiple_of(WIDE + head * HD, HD), HD)] = query_grad

    refs = (q_ref, g_ref, k_ref, v_ref, kt, vt, dk_out, dv_out)

    @pl.when(block == 0)
    def _():
        attend_block(1, EARLY_GROUPS[1], 0, refs, write)
        for read in reads:
            read.wait()

    @pl.when(block > 0)
    def _():
        dispatch(block, EARLY_GROUPS, block_range(pos_ref[0], block, docs_ref), refs, write)


def first_blocks(position, docs, q, k, v, g):
    whole = lambda rows, columns: pl.BlockSpec((rows, columns), lambda i, *_: (0, 0))
    row = lambda columns: pl.BlockSpec((BLK, columns), lambda i, *_: (i, 0))
    rows = EARLY * BLK
    return pl.pallas_call(
        first_kernel,
        grid=(EARLY,),
        in_specs=[pl.BlockSpec(memory_space=pl.ANY)] * 2 + [row(WIDE), row(WIDE), whole(rows, HD), whole(rows, HD)],
        out_specs=[row(2 * WIDE), whole(rows, HD), whole(rows, HD)],
        scratch_shapes=[pltpu.VMEM((HD, rows), jnp.bfloat16)] * 2
        + [pltpu.SMEM(position.shape, jnp.int32), pltpu.SMEM(docs.shape, jnp.int32), pltpu.SemaphoreType.DMA((2,))],
        out_shape=[
            jax.ShapeDtypeStruct((rows, 2 * WIDE), jnp.bfloat16),
            jax.ShapeDtypeStruct((rows, HD), jnp.float32),
            jax.ShapeDtypeStruct((rows, HD), jnp.float32),
        ],
        compiler_params=pltpu.CompilerParams(vmem_limit_bytes=VMEM_BYTES),
        cost_estimate=pl.CostEstimate(flops=2 * 18 * HQ * BLK * BLK * HD, bytes_accessed=8 * BLK * WIDE * 2, transcendentals=0),
        name="first_blocks",
    )(position, docs, q, g, k, v)


def rest_kernel(pos_ref, docs_ref, moved_ref, q_ref, g_ref, k_ref, v_ref, early_ref, dk0_ref, dv0_ref, *rest):
    route_ref, *parcels = rest[: 1 + len(PARCELS)]
    att_ref, dq_ref, dk_fin, dv_fin, kt, vt, dk_ref, dv_ref = rest[1 + len(PARCELS) :]
    step = pl.program_id(0)
    block = step + 1
    position = pos_ref[0]
    moved = moved_ref[position]

    @pl.when(step == 0)
    def _():
        route_ref[0] = route_of(position, moved_ref)
        route_ref[1] = moved
        kt[...] = k_ref[...].T
        vt[...] = v_ref[...].T
        dk_ref[...] = jnp.zeros_like(dk_ref)
        dv_ref[...] = jnp.zeros_like(dv_ref)
        dk_ref[: EARLY * BLK] = dk0_ref[...]
        dv_ref[: EARLY * BLK] = dv0_ref[...]
        att_ref[...] = early_ref[:, :WIDE]
        dq_ref[...] = early_ref[:, WIDE:]

    def write(head, attended, query_grad):
        here = pl.ds(pl.multiple_of(head * HD, HD), HD)
        att_ref[:, here] = attended
        dq_ref[:, here] = query_grad

    @pl.when(step > 0)
    def _():
        same = block_range(position, block, docs_ref)
        dispatch(block, GROUPS, same, (q_ref, g_ref, k_ref, v_ref, kt, vt, dk_ref, dv_ref), write)

    for at in range(EARLY, NB - 1):

        @pl.when((block == at) & (at < moved))
        def _(at=at):
            for parcel, row, line, rows, only in copies_of(at):

                @pl.when(True if only is None else moved == only)
                def _():
                    parcels[parcel][row : row + rows, :WIDE] = att_ref[line : line + rows]
                    parcels[parcel][row : row + rows, WIDE : 2 * WIDE] = dq_ref[line : line + rows]

    @pl.when(step == NB - 2)
    def _():
        for at in range(NB):
            rows = slice(at * BLK, (at + 1) * BLK)
            dk = (dk_ref[rows] * FACTOR).astype(jnp.bfloat16)
            dv = dv_ref[rows].astype(jnp.bfloat16)
            if at < NB - 1:
                if at < EARLY:
                    for turn in range(TURNS):
                        lines = slice(turn * FOLD, (turn + 1) * FOLD)
                        column = (at * TURNS + turn) * 2 * HD
                        parcels[0][BLK:, column : column + HD] = dk[lines]
                        parcels[0][BLK:, column + HD : column + 2 * HD] = dv[lines]
                else:
                    for parcel, row, line, count, only in copies_of(at):

                        @pl.when(True if only is None else moved == only)
                        def _():
                            parcels[parcel][row : row + count, 2 * WIDE : 2 * WIDE + HD] = dk[line : line + count]
                            parcels[parcel][row : row + count, 2 * WIDE + HD :] = dv[line : line + count]

            if at > 0:

                @pl.when(at >= moved)
                def _():
                    to = pl.ds(pl.multiple_of((at - moved) * BLK, BLK), BLK)
                    dk_fin[to, :] = dk
                    dv_fin[to, :] = dv


FOLD = EARLY * BLK * HD // WIDE
TURNS = BLK // FOLD
PARCEL_ROWS = (BLK + FOLD, BLK, BLK + CUT, 2 * BLK - CUT, 2 * BLK, BLK, BLK - CUT)
PARCELS = [jax.ShapeDtypeStruct((rows, 2 * WIDE + 2 * HD), jnp.bfloat16) for rows in PARCEL_ROWS]
SECOND, THIRD, OWN, RELAYED, PAIR, LAST, HALF = range(len(PARCELS))
SINGLE = len(PARCELS)
RESIDENT = 1 + OWN
LAYOUTS = {
    "cut": {
        LATE: [(OWN, 0, 0, BLK)],
        LATE + 1: [(OWN, BLK, 0, CUT), (RELAYED, 0, CUT, BLK - CUT)],
        LATE + 2: [(RELAYED, BLK - CUT, 0, BLK)],
    },
    "half": {LATE: [(OWN, 0, 0, BLK)], LATE + 1: [(OWN, BLK, 0, CUT), (HALF, 0, CUT, BLK - CUT)]},
    "whole": {LATE: [(PAIR, 0, 0, BLK)], LATE + 1: [(PAIR, BLK, 0, BLK)], LATE + 2: [(LAST, 0, 0, BLK)]},
    "single": {LATE: [(SINGLE, 0, 0, BLK)]},
}


def copies_of(at):
    if at < LATE:
        return [(SECOND if at == EARLY else THIRD, 0, 0, BLK, None)]
    places = {place for layout in ("cut", "half", "whole") for place in LAYOUTS[layout].get(at, ())}
    places = [(*place, NB - 1 if place[0] == LAST else None) for place in sorted(places)]
    return places + ([(LAST, 0, 0, BLK, LATE + 1)] if at == LATE else [])


RESULTS = [jax.ShapeDtypeStruct((ROWS, columns), jnp.bfloat16) for columns in (WIDE, WIDE, HD, HD)]


def rest_blocks(position, docs, moved, q, k, v, g, early, dk0, dv0):
    def stay(i, pos, docs, moved):
        return (jnp.maximum(i + 1 - moved[pos[0]], 0), 0)

    whole = lambda rows, columns: pl.BlockSpec((rows, columns), lambda i, *_: (0, 0))
    row = pl.BlockSpec((BLK, WIDE), lambda i, *_: (jnp.maximum(i + 1, EARLY), 0))
    early_row = pl.BlockSpec((BLK, 2 * WIDE), lambda i, *_: (1, 0))
    return pl.pallas_call(
        rest_kernel,
        grid_spec=pltpu.PrefetchScalarGridSpec(
            num_scalar_prefetch=3,
            grid=(NB - 1,),
            in_specs=[row, row, whole(ROWS, HD), whole(ROWS, HD), early_row, whole(EARLY * BLK, HD), whole(EARLY * BLK, HD)],
            out_specs=[pl.BlockSpec(memory_space=pltpu.SMEM)]
            + [whole(*parcel.shape) for parcel in PARCELS]
            + [
                pl.BlockSpec((BLK, WIDE), stay),
                pl.BlockSpec((BLK, WIDE), stay),
                whole(ROWS, HD),
                whole(ROWS, HD),
            ],
            scratch_shapes=[pltpu.VMEM((HD, ROWS), jnp.bfloat16)] * 2 + [pltpu.VMEM((ROWS, HD), jnp.float32)] * 2,
        ),
        out_shape=[jax.ShapeDtypeStruct((2,), jnp.int32)] + [pltpu.HBM(x.shape, x.dtype) for x in PARCELS] + RESULTS,
        compiler_params=pltpu.CompilerParams(vmem_limit_bytes=VMEM_BYTES),
        cost_estimate=pl.CostEstimate(flops=2 * 6 * HQ * BLK * BLK * HD * 20, bytes_accessed=8 * ROWS * WIDE, transcendentals=0),
        name="rest_blocks",
    )(position, docs, moved, q, g, k, v, early, dk0, dv0)


LANES = 8
STEPS = (1, 7, 3, 2, 6, 5)
PLAIN = NB - LATE
LARGE, BLOCK, SMALL = range(3)
RELAYS = 2 * len(STEPS)


def z_path(z, mate):
    up = (mate - z) % LANES
    if up < LANES - up:
        return sum(1 << (z + hop) % LANES for hop in range(up)), up
    return sum(1 << LANES + (z - hop) % LANES for hop in range(LANES - up)), LANES - up


def route_of(position, moved_ref):
    lane = lax.rem(position, LANES)
    base = lax.rem(position, 2 * LANES) - lane
    load = [moved_ref[base + z] for z in range(LANES)]
    free = [jnp.int32(1)] * LANES
    taken = jnp.int32(0)
    index = jnp.maximum(moved_ref[position], LATE) - LATE
    pairs = [(step, z, *z_path(z, z ^ step)) for step in STEPS for z in range(LANES)]
    for plan, most, least in ((LARGE, NB - 1, LATE), (BLOCK, NB - 1, LATE + 1), (SMALL, NB - 2, LATE + 1)):
        for step, z, links, _ in sorted(pairs, key=lambda pair: pair[3]):
            mate = z ^ step
            met = (load[z] == most) & (load[mate] <= least)
            if plan == LARGE:
                met = met & ((taken & links) == 0)
            met = jnp.where(met, free[z] * free[mate], 0)
            free[z], free[mate] = free[z] - met, free[mate] - met
            if plan == LARGE:
                taken = taken + met * links
            side = 1 if z & step & -step else 0
            mine = (met == 1) & ((lane == z) | (lane == mate))
            index = jnp.where(mine, PLAIN + plan * RELAYS + STEPS.index(step) * 2 + side, index)
    return index


def place_kernel(route_ref, *refs):
    count = 2 + len(PARCELS)
    arrived = refs[:count]
    outs = refs[count + 4 : count + 8]
    held = refs[count + 8 : count + 8 + count - RESIDENT]
    strip, small, numbers, sems_in, sems_out = refs[count + 8 + count - RESIDENT :]
    early, parcels = arrived[0], (*arrived[1:RESIDENT], *held)

    def come(which, start):
        if which == 1 + SECOND:
            copy = pltpu.make_async_copy(arrived[which].at[pl.ds(BLK, FOLD)], strip, sems_in.at[which])
        else:
            copy = pltpu.make_async_copy(arrived[which], held[which - RESIDENT], sems_in.at[which])
        if start:
            copy.start()
        else:
            copy.wait()

    read = pltpu.make_async_copy(route_ref, numbers, sems_in.at[count])
    read.start()
    for which in (1 + OWN, 1 + RELAYED, 1 + SECOND):
        come(which, True)
    read.wait()
    route, moved = numbers[0], numbers[1]
    plan = lambda at: (route >= PLAIN + at * RELAYS) & (route < PLAIN + (at + 1) * RELAYS)
    ways = {
        "cut": plan(LARGE) | (route == 1),
        "half": plan(SMALL) & (moved == LATE + 2),
        "whole": (plan(BLOCK) & (moved == LATE + 3)) | ((route > 1) & (route < PLAIN)),
        "single": (plan(BLOCK) | plan(SMALL)) & (moved == LATE + 1),
    }
    wanted = {
        1 + PAIR: ways["whole"] & (moved > LATE),
        1 + LAST: ways["whole"] & (moved > LATE + 2),
        1 + HALF: ways["half"],
        1 + SINGLE: ways["single"],
    }
    for which, needed in wanted.items():
        pl.when(needed)(functools.partial(come, which, True))
    columns = ((0, WIDE), (WIDE, WIDE), (2 * WIDE, HD), (2 * WIDE + HD, HD))

    def leave(at, way, start):
        begin = (NB - moved + at) * BLK
        pieces = []
        if at < EARLY:
            rows = pl.ds(at * BLK, BLK)
            pieces += [(slot, early.at[rows, pl.ds(slot * WIDE, WIDE)], 0, BLK) for slot in range(2)]
            pieces += [(2 + slot, small.at[rows, pl.ds(slot * HD, HD)], 0, BLK) for slot in range(2)]
        else:
            places = [place[:4] for place in copies_of(at)] if way is None else LAYOUTS[way][at]
            for parcel, row, line, rows in places:
                for slot, (column, width) in enumerate(columns):
                    pieces.append((slot, parcels[parcel].at[pl.ds(row, rows), pl.ds(column, width)], line, rows))
        for turn, (slot, source, line, rows) in enumerate(pieces):
            to = pl.ds(pl.multiple_of(begin + line, CUT), rows)
            copy = pltpu.make_async_copy(source, outs[slot].at[to], sems_out.at[at, turn])
            if start:
                copy.start()
            else:
                copy.wait()

    def each_block(blocks, start):
        for at in blocks:
            if at < LATE:
                pl.when(at < moved)(functools.partial(leave, at, None, start))
            else:
                for way, layout in LAYOUTS.items():
                    if at in layout:
                        pl.when((at < moved) & ways[way])(functools.partial(leave, at, way, start))

    each_block(range(EARLY, LATE), True)
    come(1 + SECOND, False)
    for turn in range(EARLY * TURNS):
        small[turn * FOLD : (turn + 1) * FOLD] = strip[:, turn * 2 * HD : (turn + 1) * 2 * HD]
    each_block(range(EARLY), True)
    for which in (1 + OWN, 1 + RELAYED):
        come(which, False)
    for which, needed in wanted.items():
        pl.when(needed)(functools.partial(come, which, False))
    each_block(range(LATE, NB - 1), True)
    each_block(range(NB - 1), False)


def place(route, arrived, outs):
    anywhere = pl.BlockSpec(memory_space=pl.ANY)
    arrived = [pltpu.with_memory_space_constraint(x, pltpu.VMEM) if at < RESIDENT else x for at, x in enumerate(arrived)]
    return pl.pallas_call(
        place_kernel,
        in_specs=[anywhere] * (1 + len(arrived) + 4),
        out_specs=[anywhere] * 4,
        scratch_shapes=[pltpu.VMEM(x.shape, x.dtype) for x in arrived[RESIDENT:]]
        + [
            pltpu.VMEM((FOLD, 2 * WIDE + 2 * HD), jnp.bfloat16),
            pltpu.VMEM((EARLY * BLK, 2 * HD), jnp.bfloat16),
            pltpu.SMEM(route.shape, route.dtype),
            pltpu.SemaphoreType.DMA((len(arrived) + 1,)),
            pltpu.SemaphoreType.DMA((NB - 1, 8)),
        ],
        out_shape=RESULTS,
        input_output_aliases={1 + len(arrived) + i: i for i in range(4)},
        compiler_params=pltpu.CompilerParams(vmem_limit_bytes=10 * 1024 * 1024),
        cost_estimate=pl.CostEstimate(flops=0, bytes_accessed=2 * ROWS * WIDE * 4, transcendentals=0),
        name="place_parcels",
    )(route, *arrived, *outs)


def blank_kernel(out_ref):
    del out_ref


def blank(like):
    return pl.pallas_call(
        blank_kernel,
        out_specs=pl.BlockSpec(memory_space=pl.ANY),
        out_shape=jax.ShapeDtypeStruct(like.shape, like.dtype),
        compiler_params=pltpu.CompilerParams(vmem_limit_bytes=1024 * 1024),
        name="blank",
    )()


def late_kernel(after_ref, value_ref, out_ref):
    del after_ref
    out_ref[0] = value_ref[0]


def late(after, value):
    scalar = pl.BlockSpec(memory_space=pltpu.SMEM)
    return pl.pallas_call(
        late_kernel,
        in_specs=[pl.BlockSpec(memory_space=pl.ANY), scalar],
        out_specs=scalar,
        out_shape=jax.ShapeDtypeStruct((1,), jnp.int32),
        compiler_params=pltpu.CompilerParams(vmem_limit_bytes=8 * 1024 * 1024),
        name="late",
    )(after, value)[0]


def straight_route(count, swap, *parcels):
    used = {OWN: count == 1, PAIR: count > 1, LAST: count > 2}
    sent = [lax.ppermute(x, "dp", swap) if used.get(OWN + at) else blank(x) for at, x in enumerate(parcels)]
    return (*sent, blank(PARCELS[LAST]))


def relay_route(plan, step, side, swap, *parcels):
    bit = step & -step
    heavy = [r for r, _ in swap if bool(r & bit) == bool(side)]
    relayed, straight = {LARGE: (RELAYED, OWN), BLOCK: (LAST, PAIR), SMALL: (HALF, OWN)}[plan]
    halfway = lax.ppermute(parcels[relayed - OWN], "dp", [(r, swap[r][1] ^ step) for r in heavy])
    sent = {straight: lax.ppermute(parcels[straight - OWN], "dp", [(r, swap[r][1]) for r in heavy])}
    if plan != LARGE:
        sent[SINGLE] = lax.ppermute(parcels[LAST - OWN], "dp", [pair for pair in swap if pair[0] not in heavy])
    sent[relayed] = lax.ppermute(halfway, "dp", [(r ^ step, r) for r in heavy])
    return tuple(sent[at] if at in sent else blank(PARCELS[LAST if at == SINGLE else at]) for at in range(OWN, SINGLE + 1))


def local(queries, key_rows, value_rows, out_grads, block_docs, moved_blocks):
    replicas = lax.axis_size("dp")
    swap = [(i, (i + replicas // 2) % replicas) for i in range(replicas)]
    position = lax.axis_index("dp").astype(jnp.int32).reshape(1)
    block_docs = block_docs.T
    early, dk0, dv0 = first_blocks(position, block_docs, queries, key_rows, value_rows, out_grads)
    arrived = [lax.ppermute(early, "dp", swap)]
    done = rest_blocks(position, block_docs, moved_blocks, queries, key_rows, value_rows, out_grads, early, dk0, dv0)
    route, parcels, outs = done[0], done[1 : 1 + len(PARCELS)], done[1 + len(PARCELS) :]
    arrived += [lax.ppermute(parcels[at], "dp", swap) for at in (SECOND, THIRD)]
    routes = [functools.partial(straight_route, count, swap) for count in range(PLAIN)]
    for plan in (LARGE, BLOCK, SMALL):
        routes += [functools.partial(relay_route, plan, step, side, swap) for step in STEPS for side in range(2)]
    arrived += lax.switch(late(arrived[0], route), routes, *parcels[OWN:])
    return tuple(place(route, arrived, outs))


def solution(mesh):
    placed = (P("dp", "head"), P("dp", "head"), P("dp", "head"), P("dp", "head"), P(), P())
    return jax.shard_map(
        local,
        mesh=mesh,
        in_specs=placed,
        out_specs=(P("dp", "head"), P("dp", "head"), P("dp", "head"), P("dp", "head")),
        check_vma=False,
    )
```
